32 devices in a mesh: dp: 4 (over y, core), tensor: 8 (over z, x).
Axes of the slice: x: 2, y: 2, z: 4, core: 2. Of those that a mesh axis runs over, the one named last changes fastest.
Arguments:
- token_ids: int32 [1024], P('dp'), may hold values from 0 to 128255
- attn_heads: bfloat16 [1024, 8192], P('dp', 'tensor'), may hold values from -6 to 6
- out_proj: bfloat16 [8192, 8192], P('tensor'), may hold values from -0.0625 to 0.0625
- residual: bfloat16 [1024, 8192], P(('dp', 'tensor')), may hold values from -6 to 6
- norm_gain: float32 [8192], replicated, may hold values from 0.5 to 1.5
- twist_in: bfloat16 [8192, 8192], P('dp', 'tensor'), may hold values from -0.0625 to 0.0625
- twist_out: float32 [8192], P('tensor'), may hold values from -0.26516503 to 0.26516503
- token_bias: float32 [128256], replicated, may hold values from -4 to 262
- toxicity: int32 [4], P('dp'), may hold values from 1 to 4
- prompt_len: int32 [4], P('dp'), may hold values from 1 to 128
Outputs:
- twist_vals: float32 [1024], P('dp')
- grad_in: float32 [8192, 8192], P('dp', 'tensor')
- grad_out: float32 [8192], P('tensor')
- grad_bias: float32 [128256], P('dp')
The draws below stay inside these ranges and needn't reach their ends.
All inputs are finite; a program needn't handle non-finite values.
Results may differ from the reference program's by a relative error of at most 0.033.
Values may be sent and summed in bfloat16 or wider, within the bound.
A program may use at most 128 MiB of HBM per device.

```python
import math
import jax
import jax.numpy as jnp
import numpy as np
from jax import lax

D = 8192
VOCAB = 128256
LEN = 256
ROLLOUTS = 4
TOKENS = 1024
N_DP = 4
N_TENSOR = 8


def draw_token_bias(key, part):
    key_one = jax.random.fold_in(key, 0)
    return jnp.clip(jax.random.normal(key_one, (VOCAB,), jnp.float32), -4.0, 4.0)


def with_ends(result, stream_key, least, high):
    spot = [jax.random.randint(jax.random.fold_in(stream_key, axis), (), 0, length) for axis, length in enumerate(result.shape)]
    longest = result.shape.index(max(result.shape))
    beside = spot[:longest] + [(spot[longest] + 1) % result.shape[longest]] + spot[longest + 1:]
    return result.at[tuple(spot)].set(least).at[tuple(beside)].set(high)


def shard_levels(key, dims, shards, smallest, top_value):
    def one(axis_at, parts):
        heights = jax.random.uniform(jax.random.fold_in(jax.random.fold_in(key, 6), axis_at), (parts,), jnp.float32, smallest / len(shards), top_value / len(shards))
        return jnp.repeat(jnp.exp(heights), dims[axis_at] // parts).reshape((-1,) + (1,) * (len(dims) - axis_at - 1))

    factor_of = one(*shards[0])
    for cut in shards[1:]:
        factor_of = factor_of * one(*cut)
    return factor_of


def wide_ids(rng, shape, number_of, skew):
    loads = [min(1 << octave, number_of + 1 - (1 << octave)) * (1 << 20) // math.isqrt((1 << octave) ** skew) + 1 for octave in range((number_of + 1).bit_length()) if 1 << octave <= number_of]
    scale = 1 + sum(loads) // (1 << 30)
    table = np.cumsum(np.array([max(1, weight // scale) for weight in loads]))
    ticket = jax.random.randint(jax.random.fold_in(rng, 1), shape, 0, int(table[len(loads) - 1]))
    start = jnp.left_shift(1, jnp.searchsorted(jnp.asarray(table, jnp.int32), ticket, side="right").astype(jnp.int32))
    grade = start - 1 + jax.random.randint(jax.random.fold_in(rng, 4), shape, 0, 1 << 30) % jnp.minimum(start, number_of + 1 - start)
    return jax.random.permutation(jax.random.fold_in(rng, 2), number_of)[grade].astype(jnp.int32)


def bell_draw(stream_key, shape, scale, bound, cuts=(), dtype=jnp.bfloat16):
    drawn = scale * jax.random.normal(stream_key, shape, jnp.float32)
    if cuts:
        drawn = drawn * shard_levels(stream_key, shape, cuts, -0.22, 0.18)
    return jnp.clip(drawn, -bound, bound).astype(dtype)


def setup_inputs(seed: int = 0) -> dict:
    splits = jax.random.split(jax.random.key(seed), 11)
    return {
        "token_ids": with_ends(wide_ids(splits[0], (TOKENS,), VOCAB, 2), jax.random.fold_in(splits[0], 3), 0, VOCAB - 1).astype(jnp.int32),
        "attn_heads": bell_draw(splits[1], (TOKENS, D), 1.0, 6.0, ((0, 4), (1, 8))),
        "out_proj": bell_draw(splits[2], (D, D), D ** -0.5, 0.0625, ((0, 8),)),
        "residual": bell_draw(splits[3], (TOKENS, D), 1.0, 6.0, ((0, 32),)),
        "norm_gain": jnp.clip(1.0 + 0.1 * jax.random.normal(splits[4], (D,), jnp.float32), 0.5, 1.5),
        "twist_in": bell_draw(splits[5], (D, D), D ** -0.5, 0.0625, ((0, 4), (1, 8))),
        "twist_out": bell_draw(splits[6], (D,), (4.0 / D ** 0.5), 0.26516503, ((0, 8),), jnp.float32),
        "token_bias": draw_token_bias(jax.random.fold_in(splits[10], 71), 0),
        "toxicity": with_ends(jax.random.randint(splits[8], (ROLLOUTS,), 1, 5), jax.random.fold_in(splits[8], 1), 1, 4).astype(jnp.int32),
        "prompt_len": with_ends(jax.random.randint(splits[9], (ROLLOUTS,), 1, LEN // 2 + 1), jax.random.fold_in(splits[9], 1), 1, (LEN // 2 + 1) - 1).astype(jnp.int32),
    }


def normalize(hidden, norm_gain):
    values = hidden.astype(jnp.float32)
    scaled = lax.rsqrt(lax.optimization_barrier(jnp.mean(values * values, axis=-1, keepdims=True)) + 1e-05)
    return (values * scaled * norm_gain[None, :]).astype(jnp.bfloat16)

def reference(token_ids, attn_heads, out_proj, residual, norm_gain, twist_in, twist_out, token_bias, toxicity, prompt_len):
    block_width = D // N_TENSOR
    tok_count = attn_heads.shape[0]
    head_blocks = attn_heads.reshape(tok_count, N_TENSOR, block_width).transpose(1, 0, 2)
    proj_blocks = out_proj.reshape(N_TENSOR, block_width, D)

    def add_block(accum, pair):
        partial_sum = jnp.dot(pair[0], pair[1], preferred_element_type=jnp.float32).astype(jnp.bfloat16)
        partial_sum = lax.optimization_barrier(partial_sum)
        return (accum + partial_sum.astype(jnp.float32), None)
    summed, unused = lax.scan(add_block, jnp.zeros((tok_count, D), jnp.float32), (head_blocks, proj_blocks))
    hidden = (residual.astype(jnp.float32) + summed).astype(jnp.bfloat16)
    normed = normalize(hidden, norm_gain)
    pre_act = jnp.dot(normed, twist_in, preferred_element_type=jnp.float32)
    active = jax.nn.silu(pre_act)
    twist_vals = jnp.dot(active, twist_out, precision=lax.Precision.HIGHEST) + token_bias[token_ids]
    grid = twist_vals.reshape(N_DP, LEN)
    live = jnp.arange(LEN)[None, :] >= prompt_len[:, None]
    levels = toxicity.astype(jnp.float32)[:, None] * live.astype(jnp.float32)
    highest = lax.optimization_barrier(jnp.max(jnp.where(live, grid, -1e+30), axis=0))
    expo = jnp.where(live, jnp.exp(jnp.where(live, grid - highest[None, :], -80.0)), 0.0)
    totals = lax.optimization_barrier(jnp.sum(expo, axis=0))
    lab_sum = lax.optimization_barrier(jnp.sum(levels, axis=0))
    weights = (expo / jnp.maximum(totals, 1.0)[None, :] - levels / jnp.maximum(lab_sum, 1.0)[None, :]) / LEN
    flat = weights.reshape(-1)
    grad_out = jnp.dot(flat, active, precision=lax.Precision.HIGHEST)
    grad_bias = jax.ops.segment_sum(flat, token_ids, num_segments=VOCAB)
    sigma = jax.nn.sigmoid(pre_act)
    d_pre = (flat[:, None] * twist_out[None, :] * sigma * (1.0 + pre_act * (1.0 - sigma))).astype(jnp.bfloat16)
    grad_in = jnp.dot(normed.T, d_pre, preferred_element_type=jnp.float32)
    return (twist_vals, grad_in, grad_out, grad_bias)
```

```python
import jax
import jax.numpy as jnp
from jax import lax
from jax.sharding import PartitionSpec as P


def normalize(hidden, norm_gain):
    values = hidden.astype(jnp.float32)
    scaled = lax.rsqrt(jnp.mean(values * values, axis=-1, keepdims=True) + 1e-05)
    return (values * scaled * norm_gain[None, :]).astype(jnp.bfloat16)


def make_local(n_dp, n_tensor):
    def local(
        token_ids,
        attn_heads,
        out_proj,
        residual,
        norm_gain,
        twist_in,
        twist_out,
        token_bias,
        toxicity,
        prompt_len,
    ):
        seq_len = attn_heads.shape[0]
        rows = residual.shape[0]
        vocab_size = token_bias.shape[0]
        width = attn_heads.shape[1] * n_tensor
        feats = width // n_dp
        tokens = seq_len * n_dp
        me = lax.axis_index("dp")

        ids_all = lax.all_gather(
            jnp.concatenate([token_ids, toxicity, prompt_len]), "dp", axis=0
        )
        levels_all = ids_all[:, seq_len].astype(jnp.float32)
        prompt_all = ids_all[:, seq_len + 1]
        ids_all = ids_all[:, :seq_len]

        partial_sum = jnp.dot(attn_heads, out_proj, preferred_element_type=jnp.float32)
        summed = lax.psum_scatter(
            partial_sum.astype(jnp.bfloat16), "tensor", scatter_dimension=0, tiled=True
        ).astype(jnp.float32)
        hidden = (residual.astype(jnp.float32) + summed).astype(jnp.bfloat16)
        normed = normalize(hidden, norm_gain)
        split = lax.all_to_all(normed, "dp", split_axis=1, concat_axis=0, tiled=True)
        columns = lax.all_gather(split, "tensor", axis=0, tiled=True)
        pre_part = jnp.dot(columns, twist_in, preferred_element_type=jnp.float32)
        pre_act = lax.psum_scatter(
            pre_part.astype(jnp.bfloat16), "dp", scatter_dimension=0, tiled=True
        ).astype(jnp.float32)
        sigma = jax.nn.sigmoid(pre_act)
        active = pre_act * sigma
        slope = (twist_out[None, :] * sigma * (1.0 + pre_act * (1.0 - sigma))).astype(jnp.bfloat16)
        slope_all = lax.all_gather(slope, "dp", axis=0, tiled=True)

        span = seq_len // n_dp
        blocks = span // rows
        own_ids = lax.dynamic_slice_in_dim(ids_all, me * span, span, axis=1)
        psi = lax.psum(jnp.sum(active * twist_out[None, :], axis=1), "tensor")
        grid = psi.reshape(blocks, n_dp, rows).transpose(1, 0, 2).reshape(n_dp, span)
        grid = grid + token_bias[own_ids]
        live = (me * span + jnp.arange(span))[None, :] >= prompt_all[:, None]
        levels = levels_all[:, None] * live.astype(jnp.float32)
        highest = jnp.max(jnp.where(live, grid, -1e30), axis=0)
        expo = jnp.where(live, jnp.exp(jnp.where(live, grid - highest[None, :], -80.0)), 0.0)
        totals = jnp.sum(expo, axis=0)
        lab_sum = jnp.sum(levels, axis=0)
        weights = (
            expo / jnp.maximum(totals, 1.0)[None, :] - levels / jnp.maximum(lab_sum, 1.0)[None, :]
        ) / seq_len
        flat = weights.reshape(n_dp, blocks, rows).transpose(1, 0, 2).reshape(-1)
        grad_out_part = jnp.sum(flat[:, None] * active, axis=0)
        packed = jnp.concatenate([flat, grid.reshape(-1), grad_out_part])
        packed = lax.all_gather(packed, "dp", axis=0)
        flat_all = packed[:, :seq_len].reshape(tokens)
        grids = packed[:, seq_len : 2 * seq_len].reshape(n_dp, n_dp, span)
        twist_vals = lax.dynamic_index_in_dim(grids, me, 1, keepdims=False).reshape(seq_len)
        grad_out = jnp.sum(packed[:, 2 * seq_len :], axis=0)

        d_pre = (slope_all.astype(jnp.float32) * flat_all[:, None]).astype(jnp.bfloat16)
        contract = (((0,), (0,)), ((), ()))
        grad_in = lax.dot_general(columns, d_pre, contract, preferred_element_type=jnp.float32)

        own_vocab = vocab_size // n_dp
        ids_perm = ids_all.reshape(n_dp, n_tensor, rows).transpose(1, 0, 2).reshape(-1)
        spot = ids_perm - me * own_vocab
        spot = jnp.where((spot >= 0) & (spot < own_vocab), spot, own_vocab)
        grad_bias = jnp.zeros((own_vocab,), jnp.float32).at[spot].add(flat_all, mode="drop")
        return (twist_vals, grad_in, grad_out, grad_bias)

    return local


def solution(mesh):
    placed = (
        P("dp"),
        P("dp", "tensor"),
        P("tensor", None),
        P(("dp", "tensor"), None),
        P(),
        P("dp", "tensor"),
        P("tensor"),
        P(),
        P("dp"),
        P("dp"),
    )
    return jax.shard_map(
        make_local(mesh.shape["dp"], mesh.shape["tensor"]),
        mesh=mesh,
        in_specs=placed,
        out_specs=(P("dp"), P("dp", "tensor"), P("tensor"), P("dp")),
        check_vma=False,
    )
```

```python
import functools

import jax
import jax.numpy as jnp
from jax import lax
from jax.experimental import pallas as pl
from jax.experimental.pallas import tpu as pltpu
from jax.sharding import PartitionSpec as P

PIECES = 2
MESH = pl.DeviceIdType.MESH


def ring_kernel(
    n_dp,
    n,
    part_ref,
    resid_ref,
    gain_ref,
    twist_ref,
    pre_ref,
    cols_ref,
    slots,
    hid,
    normed,
    outbox,
    inbox,
    sum_send,
    sum_recv,
    swap_send,
    swap_recv,
    ring_send,
    ring_recv,
    pre_send,
    pre_recv,
):
    rows, width = resid_ref.shape
    feats = width // n_dp
    half = n_dp // 2
    per = n // n_dp
    piece = width // (2 * PIECES)
    me = lax.axis_index("dp")
    t_me = lax.axis_index("tensor")

    def spot_of(t):
        return jnp.where(t % 2 == 0, t // 2, n - 1 - t // 2)

    def index_of(p):
        p = lax.rem(p + 2 * n, n)
        return jnp.where(p < n // 2, 2 * p, 2 * (n - 1 - p) + 1)

    p = spot_of(t_me)
    near = (index_of(p + 1), index_of(p - 1))
    back = (-1, 1)

    barrier = pltpu.get_barrier_semaphore()
    for t in near:
        pl.semaphore_signal(barrier, inc=1, device_id=(me, t), device_id_type=MESH)
    for step in range(1, n_dp):
        peer = lax.rem(me + step, n_dp)
        pl.semaphore_signal(barrier, inc=1, device_id=(peer, t_me), device_id_type=MESH)
    pl.semaphore_wait(barrier, n_dp + 1)

    def span(way, q):
        return pl.ds((way * PIECES + q) * piece, piece)

    def sum_copy(way, q, step, first):
        if first:
            source = part_ref.at[index_of(p + back[way]), :, span(way, q)]
        else:
            source = slots.at[way, q, step - 1]
        return pltpu.make_async_remote_copy(
            src_ref=source,
            dst_ref=slots.at[way, q, step],
            send_sem=sum_send.at[way, q, step],
            recv_sem=sum_recv.at[way, q, step],
            device_id=(me, near[way]),
            device_id_type=MESH,
        )

    for q in range(PIECES):
        for way in range(2):
            sum_copy(way, q, 0, True).start()

    def sum_step(step, carry):
        for q in range(PIECES):
            for way in range(2):
                sum_copy(way, q, step - 1, True).wait_recv()
                t = index_of(p + back[way] * (step + 1))
                mine = part_ref[t, :, span(way, q)].astype(jnp.float32)
                so_far = slots[way, q, step - 1].astype(jnp.float32)
                slots[way, q, step - 1] = (so_far + mine).astype(jnp.bfloat16)
                sum_copy(way, q, step, False).start()
        return carry

    lax.fori_loop(1, n - 1, sum_step, 0)
    for q in range(PIECES):
        for way in range(2):
            sum_copy(way, q, n - 2, True).wait_recv()
            mine = part_ref[t_me, :, span(way, q)].astype(jnp.float32)
            so_far = slots[way, q, n - 2].astype(jnp.float32)
            total = resid_ref[:, span(way, q)].astype(jnp.float32) + (so_far + mine)
            hid[:, span(way, q)] = total.astype(jnp.bfloat16)

    squares = jnp.zeros((rows, 1), jnp.float32)
    for i in range(n_dp):
        values = hid[:, pl.ds(i * feats, feats)].astype(jnp.float32)
        squares = squares + jnp.sum(values * values, axis=1, keepdims=True)
    scaled = lax.rsqrt(squares / width + 1e-05)
    for i in range(n_dp):
        values = hid[:, pl.ds(i * feats, feats)].astype(jnp.float32)
        gains = gain_ref[:, pl.ds(i * feats, feats)]
        normed[i] = (values * scaled * gains).astype(jnp.bfloat16)

    def swap_copy(peer, source):
        return pltpu.make_async_remote_copy(
            src_ref=normed.at[peer],
            dst_ref=cols_ref.at[t_me, source],
            send_sem=swap_send.at[peer],
            recv_sem=swap_recv.at[source],
            device_id=(peer, t_me),
            device_id_type=MESH,
        )

    for step in range(1, n_dp):
        peer = lax.rem(me + step, n_dp)
        swap_copy(peer, me).start()
    cols_ref[t_me, me] = normed[me]
    for step in range(1, n_dp):
        peer = lax.rem(me + step, n_dp)
        swap_copy(peer, peer).wait_recv()

    def ring_copy(way, step):
        t = index_of(p + back[way] * step)
        place = cols_ref.at[t, pl.ds(way * half, half)]
        return pltpu.make_async_remote_copy(
            src_ref=place,
            dst_ref=place,
            send_sem=ring_send.at[way, step],
            recv_sem=ring_recv.at[way, step],
            device_id=(me, near[way]),
            device_id_type=MESH,
        )

    def pre_copy(t, way, source):
        owner = t // per
        local = lax.rem(t, per)
        return pltpu.make_async_remote_copy(
            src_ref=outbox.at[t, way],
            dst_ref=inbox.at[source, local, way],
            send_sem=pre_send.at[t, way],
            recv_sem=pre_recv.at[source, local, way],
            device_id=(owner, t_me),
            device_id_type=MESH,
        )

    def multiply(t, way):
        block = cols_ref[t, pl.ds(way * half, half)].reshape(half * rows, feats)
        found = jnp.dot(block, twist_ref[...], preferred_element_type=jnp.float32)
        outbox[t, way] = found.astype(jnp.bfloat16)
        owner = t // per

        @pl.when(owner != me)
        def _():
            pre_copy(t, way, me).start()

    def ring_step(step, carry):
        for way in range(2):

            @pl.when(step > 0)
            def _():
                before = ring_copy(way, step - 1)
                before.wait_recv()

            @pl.when(step < n - 1)
            def _():
                ring_copy(way, step).start()

        for way in range(2):
            multiply(index_of(p + back[way] * step), way)
        return carry

    lax.fori_loop(0, n, ring_step, 0)

    for local in range(per):
        for way in range(2):
            total = outbox[me * per + local, way].astype(jnp.float32)
            for step in range(1, n_dp):
                peer = lax.rem(me + step, n_dp)
                pre_copy(me * per + local, way, peer).wait_recv()
                total = total + inbox[peer, local, way].astype(jnp.float32)
            pre_ref[local, way] = total

    for step in range(1, n_dp):
        peer = lax.rem(me + step, n_dp)
        swap_copy(peer, me).wait_send()
        for local in range(per):
            for way in range(2):
                pre_copy(peer * per + local, way, me).wait_send()

    def finish(step, carry):
        for way in range(2):
            for q in range(PIECES):
                sum_copy(way, q, step, True).wait_send()
            ring_copy(way, step).wait_send()
        return carry

    lax.fori_loop(0, n - 1, finish, 0)


def ring_call(n_dp, n, part, resid, gain, twist):
    rows, width = resid.shape
    feats, units = twist.shape
    half, per = n_dp // 2, n // n_dp
    piece = width // (2 * PIECES)
    dma = pltpu.SemaphoreType.DMA
    vmem = pl.BlockSpec(memory_space=pltpu.VMEM)
    pre_act, columns = pl.pallas_call(
        functools.partial(ring_kernel, n_dp, n),
        out_shape=(
            jax.ShapeDtypeStruct((per, 2, half * rows, units), jnp.float32),
            jax.ShapeDtypeStruct((n, n_dp, rows, feats), jnp.bfloat16),
        ),
        in_specs=[vmem] * 4,
        out_specs=(vmem, vmem),
        scratch_shapes=[
            pltpu.VMEM((2, PIECES, n - 1, rows, piece), jnp.bfloat16),
            pltpu.VMEM((rows, width), jnp.bfloat16),
            pltpu.VMEM((n_dp, rows, feats), jnp.bfloat16),
            pltpu.VMEM((n, 2, half * rows, units), jnp.bfloat16),
            pltpu.VMEM((n_dp, per, 2, half * rows, units), jnp.bfloat16),
            dma((2, PIECES, n - 1)),
            dma((2, PIECES, n - 1)),
            dma((n_dp,)),
            dma((n_dp,)),
            dma((2, n - 1)),
            dma((2, n - 1)),
            dma((n, 2)),
            dma((n_dp, per, 2)),
        ],
        compiler_params=pltpu.CompilerParams(
            collective_id=0, has_side_effects=True, vmem_limit_bytes=44 * 1024 * 1024
        ),
    )(part.reshape(n, rows, width), resid, gain.reshape(1, width), twist)
    return pre_act.reshape(per * n_dp * rows, units), columns.reshape(n * n_dp * rows, feats)


def make_local(n_dp, n_tensor):
    def local(
        token_ids,
        attn_heads,
        out_proj,
        residual,
        norm_gain,
        twist_in,
        twist_out,
        token_bias,
        toxicity,
        prompt_len,
    ):
        seq_len = attn_heads.shape[0]
        rows = residual.shape[0]
        vocab_size = token_bias.shape[0]
        tokens = seq_len * n_dp
        me = lax.axis_index("dp")

        ids_all = lax.all_gather(
            jnp.concatenate([token_ids, toxicity, prompt_len]), "dp", axis=0
        )
        levels_all = ids_all[:, seq_len].astype(jnp.float32)
        prompt_all = ids_all[:, seq_len + 1]
        ids_all = ids_all[:, :seq_len]

        partial_sum = jnp.dot(attn_heads, out_proj, preferred_element_type=jnp.float32)
        pre_act, columns = ring_call(
            n_dp, n_tensor, partial_sum.astype(jnp.bfloat16), residual, norm_gain, twist_in
        )
        sigma = jax.nn.sigmoid(pre_act)
        active = pre_act * sigma
        slope = (twist_out[None, :] * sigma * (1.0 + pre_act * (1.0 - sigma))).astype(jnp.bfloat16)
        slope_all = lax.all_gather(slope, "dp", axis=0, tiled=True)

        span = seq_len // n_dp
        blocks = span // rows
        own_ids = lax.dynamic_slice_in_dim(ids_all, me * span, span, axis=1)
        psi = lax.psum(jnp.sum(active * twist_out[None, :], axis=1), "tensor")
        grid = psi.reshape(blocks, n_dp, rows).transpose(1, 0, 2).reshape(n_dp, span)
        grid = grid + token_bias[own_ids]
        live = (me * span + jnp.arange(span))[None, :] >= prompt_all[:, None]
        levels = levels_all[:, None] * live.astype(jnp.float32)
        highest = jnp.max(jnp.where(live, grid, -1e30), axis=0)
        expo = jnp.where(live, jnp.exp(jnp.where(live, grid - highest[None, :], -80.0)), 0.0)
        totals = jnp.sum(expo, axis=0)
        lab_sum = jnp.sum(levels, axis=0)
        weights = (
            expo / jnp.maximum(totals, 1.0)[None, :] - levels / jnp.maximum(lab_sum, 1.0)[None, :]
        ) / seq_len
        flat = weights.reshape(n_dp, blocks, rows).transpose(1, 0, 2).reshape(-1)
        grad_out_part = jnp.sum(flat[:, None] * active, axis=0)
        packed = jnp.concatenate([flat, grid.reshape(-1), grad_out_part])
        packed = lax.all_gather(packed, "dp", axis=0)
        flat_all = packed[:, :seq_len].reshape(tokens)
        grids = packed[:, seq_len : 2 * seq_len].reshape(n_dp, n_dp, span)
        twist_vals = lax.dynamic_index_in_dim(grids, me, 1, keepdims=False).reshape(seq_len)
        grad_out = jnp.sum(packed[:, 2 * seq_len :], axis=0)

        d_pre = (slope_all.astype(jnp.float32) * flat_all[:, None]).astype(jnp.bfloat16)
        contract = (((0,), (0,)), ((), ()))
        grad_in = lax.dot_general(columns, d_pre, contract, preferred_element_type=jnp.float32)

        own_vocab = vocab_size // n_dp
        ids_perm = ids_all.reshape(n_dp, n_tensor, rows).transpose(1, 0, 2).reshape(-1)
        spot = ids_perm - me * own_vocab
        spot = jnp.where((spot >= 0) & (spot < own_vocab), spot, own_vocab)
        grad_bias = jnp.zeros((own_vocab,), jnp.float32).at[spot].add(flat_all, mode="drop")
        return (twist_vals, grad_in, grad_out, grad_bias)

    return local


def solution(mesh):
    placed = (
        P("dp"),
        P("dp", "tensor"),
        P("tensor", None),
        P(("dp", "tensor"), None),
        P(),
        P("dp", "tensor"),
        P("tensor"),
        P(),
        P("dp"),
        P("dp"),
    )
    return jax.shard_map(
        make_local(mesh.shape["dp"], mesh.shape["tensor"]),
        mesh=mesh,
        in_specs=placed,
        out_specs=(P("dp"), P("dp", "tensor"), P("tensor"), P("dp")),
        check_vma=False,
    )
```

```python
import functools

import jax
import jax.numpy as jnp
from jax import lax
from jax.experimental import pallas as pl
from jax.experimental.pallas import tpu as pltpu
from jax.sharding import PartitionSpec as P

PIECES = 2
MESH = pl.DeviceIdType.MESH


def ring_kernel(
    n_dp,
    n,
    part_ref,
    resid_ref,
    gain_ref,
    twist_ref,
    head_ref,
    meta_ref,
    act_ref,
    cols_ref,
    slope_ref,
    psi_ref,
    metas_ref,
    slots,
    hid,
    normed,
    outbox,
    inbox,
    psi_box,
    sum_send,
    sum_recv,
    swap_send,
    swap_recv,
    ring_send,
    ring_recv,
    pre_send,
    pre_recv,
    meta_send,
    meta_recv,
    slope_send,
    slope_recv,
    psi_send,
    psi_recv,
):
    rows, width = resid_ref.shape
    feats = width // n_dp
    half = n_dp // 2
    per = n // n_dp
    piece = width // (2 * PIECES)
    block = half * rows
    me = lax.axis_index("dp")
    t_me = lax.axis_index("tensor")

    def spot_of(t):
        return jnp.where(t % 2 == 0, t // 2, n - 1 - t // 2)

    def index_of(p):
        p = lax.rem(p + 2 * n, n)
        return jnp.where(p < n // 2, 2 * p, 2 * (n - 1 - p) + 1)

    p = spot_of(t_me)
    near = (index_of(p + 1), index_of(p - 1))
    back = (-1, 1)

    barrier = pltpu.get_barrier_semaphore()
    for step in range(1, n):
        t = lax.rem(t_me + step, n)
        pl.semaphore_signal(barrier, inc=1, device_id=(me, t), device_id_type=MESH)
    for step in range(1, n_dp):
        peer = lax.rem(me + step, n_dp)
        pl.semaphore_signal(barrier, inc=1, device_id=(peer, t_me), device_id_type=MESH)
    pl.semaphore_wait(barrier, n_dp + n - 2)

    def span(way, q):
        return pl.ds((way * PIECES + q) * piece, piece)

    def sum_copy(way, q, step, first):
        if first:
            source = part_ref.at[index_of(p + back[way]), :, span(way, q)]
        else:
            source = slots.at[way, q, step - 1]
        return pltpu.make_async_remote_copy(
            src_ref=source,
            dst_ref=slots.at[way, q, step],
            send_sem=sum_send.at[way, q, step],
            recv_sem=sum_recv.at[way, q, step],
            device_id=(me, near[way]),
            device_id_type=MESH,
        )

    for q in range(PIECES):
        for way in range(2):
            sum_copy(way, q, 0, True).start()

    def meta_copy(peer, source):
        return pltpu.make_async_remote_copy(
            src_ref=meta_ref,
            dst_ref=metas_ref.at[source],
            send_sem=meta_send.at[peer],
            recv_sem=meta_recv.at[source],
            device_id=(peer, t_me),
            device_id_type=MESH,
        )

    for step in range(1, n_dp):
        meta_copy(lax.rem(me + step, n_dp), me).start()
    metas_ref[me] = meta_ref[...]

    def sum_step(step, carry):
        for q in range(PIECES):
            for way in range(2):
                sum_copy(way, q, step - 1, True).wait_recv()
                t = index_of(p + back[way] * (step + 1))
                mine = part_ref[t, :, span(way, q)].astype(jnp.float32)
                so_far = slots[way, q, step - 1].astype(jnp.float32)
                slots[way, q, step - 1] = (so_far + mine).astype(jnp.bfloat16)
                sum_copy(way, q, step, False).start()
        return carry

    lax.fori_loop(1, n - 1, sum_step, 0)
    for q in range(PIECES):
        for way in range(2):
            sum_copy(way, q, n - 2, True).wait_recv()
            mine = part_ref[t_me, :, span(way, q)].astype(jnp.float32)
            so_far = slots[way, q, n - 2].astype(jnp.float32)
            total = resid_ref[:, span(way, q)].astype(jnp.float32) + (so_far + mine)
            hid[:, span(way, q)] = total.astype(jnp.bfloat16)

    squares = jnp.zeros((rows, 1), jnp.float32)
    for i in range(n_dp):
        values = hid[:, pl.ds(i * feats, feats)].astype(jnp.float32)
        squares = squares + jnp.sum(values * values, axis=1, keepdims=True)
    scaled = lax.rsqrt(squares / width + 1e-05)
    for i in range(n_dp):
        values = hid[:, pl.ds(i * feats, feats)].astype(jnp.float32)
        gains = gain_ref[:, pl.ds(i * feats, feats)]
        normed[i] = (values * scaled * gains).astype(jnp.bfloat16)

    def swap_copy(peer, source):
        return pltpu.make_async_remote_copy(
            src_ref=normed.at[peer],
            dst_ref=cols_ref.at[t_me, source],
            send_sem=swap_send.at[peer],
            recv_sem=swap_recv.at[source],
            device_id=(peer, t_me),
            device_id_type=MESH,
        )

    for step in range(1, n_dp):
        peer = lax.rem(me + step, n_dp)
        swap_copy(peer, me).start()
    cols_ref[t_me, me] = normed[me]
    for step in range(1, n_dp):
        peer = lax.rem(me + step, n_dp)
        swap_copy(peer, peer).wait_recv()

    def ring_copy(way, step, i):
        t = index_of(p + back[way] * step)
        place = cols_ref.at[t, way * half + i]
        return pltpu.make_async_remote_copy(
            src_ref=place,
            dst_ref=place,
            send_sem=ring_send.at[way, step, i],
            recv_sem=ring_recv.at[way, step, i],
            device_id=(me, near[way]),
            device_id_type=MESH,
        )

    def pre_copy(t, way, source):
        owner = t // per
        local = lax.rem(t, per)
        return pltpu.make_async_remote_copy(
            src_ref=outbox.at[t, way],
            dst_ref=inbox.at[source, local, way],
            send_sem=pre_send.at[t, way],
            recv_sem=pre_recv.at[source, local, way],
            device_id=(owner, t_me),
            device_id_type=MESH,
        )

    def multiply(t, way):
        found = cols_ref[t, pl.ds(way * half, half)].reshape(block, feats)
        found = jnp.dot(found, twist_ref[...], preferred_element_type=jnp.float32)
        outbox[t, way] = found.astype(jnp.bfloat16)
        owner = t // per

        @pl.when(owner != me)
        def _():
            pre_copy(t, way, me).start()

    def ring_step(step, carry):
        for i in range(half):
            for way in range(2):

                @pl.when(step > 0)
                def _():
                    ring_copy(way, step - 1, i).wait_recv()

                @pl.when(step < n - 1)
                def _():
                    ring_copy(way, step, i).start()

        for way in range(2):
            multiply(index_of(p + back[way] * step), way)
        return carry

    lax.fori_loop(0, n, ring_step, 0)

    for local in range(per):
        for way in range(2):
            total = outbox[me * per + local, way].astype(jnp.float32)
            for step in range(1, n_dp):
                peer = lax.rem(me + step, n_dp)
                pre_copy(me * per + local, way, peer).wait_recv()
                total = total + inbox[peer, local, way].astype(jnp.float32)
            sigma = 1.0 / (1.0 + jnp.exp(-total))
            act_ref[pl.ds((local * 2 + way) * block, block)] = total * sigma
            slope = head_ref[0:1, :] * sigma * (1.0 + total * (1.0 - sigma))
            slope_ref[me, local, way] = slope.astype(jnp.bfloat16)

    twin = me + 1 - 2 * lax.rem(me, 2)

    def slope_copy(peer, owner):
        return pltpu.make_async_remote_copy(
            src_ref=slope_ref.at[owner],
            dst_ref=slope_ref.at[owner],
            send_sem=slope_send.at[peer, owner],
            recv_sem=slope_recv.at[owner],
            device_id=(peer, t_me),
            device_id_type=MESH,
        )

    for step in range(2, n_dp, 2):
        slope_copy(lax.rem(me + step, n_dp), me).start()
    slope_copy(twin, me).start()

    psi_box[t_me] = lax.dot_general(
        head_ref[...],
        act_ref[...],
        (((1,), (1,)), ((), ())),
        precision=lax.Precision.HIGHEST,
        preferred_element_type=jnp.float32,
    )

    def psi_copy(peer, source):
        return pltpu.make_async_remote_copy(
            src_ref=psi_box.at[t_me],
            dst_ref=psi_box.at[source],
            send_sem=psi_send.at[peer],
            recv_sem=psi_recv.at[source],
            device_id=(me, peer),
            device_id_type=MESH,
        )

    for step in range(1, n):
        psi_copy(lax.rem(t_me + step, n), t_me).start()
    for step in range(1, n):
        t = lax.rem(t_me + step, n)
        psi_copy(t, t).wait_recv()
    total = psi_box[0]
    for t in range(1, n):
        total = total + psi_box[t]
    psi_ref[...] = total

    for step in range(2, n_dp, 2):
        peer = lax.rem(me + step, n_dp)
        slope_copy(peer, peer).wait_recv()
        slope_copy(twin, peer).start()
    slope_copy(twin, twin).wait_recv()
    for step in range(2, n_dp, 2):
        peer = lax.rem(twin + step, n_dp)
        slope_copy(twin, peer).wait_recv()

    for step in range(2, n_dp, 2):
        peer = lax.rem(me + step, n_dp)
        slope_copy(peer, me).wait_send()
        slope_copy(twin, peer).wait_send()
    slope_copy(twin, me).wait_send()
    for step in range(1, n):
        psi_copy(lax.rem(t_me + step, n), t_me).wait_send()
    for step in range(1, n_dp):
        peer = lax.rem(me + step, n_dp)
        meta_copy(peer, me).wait_send()
        meta_copy(peer, peer).wait_recv()

    for step in range(1, n_dp):
        peer = lax.rem(me + step, n_dp)
        swap_copy(peer, me).wait_send()
        for local in range(per):
            for way in range(2):
                pre_copy(peer * per + local, way, me).wait_send()

    def finish(step, carry):
        for way in range(2):
            for q in range(PIECES):
                sum_copy(way, q, step, True).wait_send()
            for i in range(half):
                ring_copy(way, step, i).wait_send()
        return carry

    lax.fori_loop(0, n - 1, finish, 0)


def ring_call(n_dp, n, part, resid, gain, twist, head, meta):
    rows, width = resid.shape
    feats, units = twist.shape
    half, per = n_dp // 2, n // n_dp
    span = per * n_dp * rows
    piece = width // (2 * PIECES)
    dma = pltpu.SemaphoreType.DMA
    vmem = pl.BlockSpec(memory_space=pltpu.VMEM)
    active, columns, slope, psi, metas = pl.pallas_call(
        functools.partial(ring_kernel, n_dp, n),
        out_shape=(
            jax.ShapeDtypeStruct((span, units), jnp.float32),
            jax.ShapeDtypeStruct((n, n_dp, rows, feats), jnp.bfloat16),
            jax.ShapeDtypeStruct((n_dp, per, 2, half * rows, units), jnp.bfloat16),
            jax.ShapeDtypeStruct((8, span), jnp.float32),
            jax.ShapeDtypeStruct((n_dp,) + meta.shape, jnp.int32),
        ),
        in_specs=[vmem] * 6,
        out_specs=(vmem,) * 5,
        scratch_shapes=[
            pltpu.VMEM((2, PIECES, n - 1, rows, piece), jnp.bfloat16),
            pltpu.VMEM((rows, width), jnp.bfloat16),
            pltpu.VMEM((n_dp, rows, feats), jnp.bfloat16),
            pltpu.VMEM((n, 2, half * rows, units), jnp.bfloat16),
            pltpu.VMEM((n_dp, per, 2, half * rows, units), jnp.bfloat16),
            pltpu.VMEM((n, 8, span), jnp.float32),
            dma((2, PIECES, n - 1)),
            dma((2, PIECES, n - 1)),
            dma((n_dp,)),
            dma((n_dp,)),
            dma((2, n - 1, half)),
            dma((2, n - 1, half)),
            dma((n, 2)),
            dma((n_dp, per, 2)),
            dma((n_dp,)),
            dma((n_dp,)),
            dma((n_dp, n_dp)),
            dma((n_dp,)),
            dma((n,)),
            dma((n,)),
        ],
        compiler_params=pltpu.CompilerParams(
            collective_id=0, has_side_effects=True, vmem_limit_bytes=44 * 1024 * 1024
        ),
    )(
        part.reshape(n, rows, width),
        resid,
        gain.reshape(1, width),
        twist,
        jnp.broadcast_to(head[None, :], (8, units)),
        meta,
    )
    columns = columns.reshape(n * n_dp * rows, feats)
    return active, columns, slope.reshape(n_dp * span, units), psi[0], metas.reshape(n_dp, -1)


def make_local(n_dp, n_tensor):
    def local(
        token_ids,
        attn_heads,
        out_proj,
        residual,
        norm_gain,
        twist_in,
        twist_out,
        token_bias,
        toxicity,
        prompt_len,
    ):
        seq_len = attn_heads.shape[0]
        rows = residual.shape[0]
        vocab_size = token_bias.shape[0]
        tokens = seq_len * n_dp
        me = lax.axis_index("dp")

        meta = jnp.concatenate([token_ids, toxicity, prompt_len])
        meta = jnp.pad(meta, (0, -meta.shape[0] % 1024)).reshape(-1, 128)

        partial_sum = jnp.dot(attn_heads, out_proj, preferred_element_type=jnp.float32)
        active, columns, slope_all, psi, metas = ring_call(
            n_dp,
            n_tensor,
            partial_sum.astype(jnp.bfloat16),
            residual,
            norm_gain,
            twist_in,
            twist_out,
            meta,
        )
        levels_all = metas[:, seq_len].astype(jnp.float32)
        prompt_all = metas[:, seq_len + 1]
        ids_all = metas[:, :seq_len]

        span = seq_len // n_dp
        blocks = span // rows
        own_ids = lax.dynamic_slice_in_dim(ids_all, me * span, span, axis=1)
        grid = psi.reshape(blocks, n_dp, rows).transpose(1, 0, 2).reshape(n_dp, span)
        grid = grid + token_bias[own_ids]
        live = (me * span + jnp.arange(span))[None, :] >= prompt_all[:, None]
        levels = levels_all[:, None] * live.astype(jnp.float32)
        highest = jnp.max(jnp.where(live, grid, -1e30), axis=0)
        expo = jnp.where(live, jnp.exp(jnp.where(live, grid - highest[None, :], -80.0)), 0.0)
        totals = jnp.sum(expo, axis=0)
        lab_sum = jnp.sum(levels, axis=0)
        weights = (
            expo / jnp.maximum(totals, 1.0)[None, :] - levels / jnp.maximum(lab_sum, 1.0)[None, :]
        ) / seq_len
        flat = weights.reshape(n_dp, blocks, rows).transpose(1, 0, 2).reshape(-1)
        grad_out_part = jnp.sum(flat[:, None] * active, axis=0)
        packed = jnp.concatenate([flat, grid.reshape(-1), grad_out_part])
        packed = lax.all_gather(packed, "dp", axis=0)
        flat_all = packed[:, :seq_len].reshape(tokens)
        grids = packed[:, seq_len : 2 * seq_len].reshape(n_dp, n_dp, span)
        twist_vals = lax.dynamic_index_in_dim(grids, me, 1, keepdims=False).reshape(seq_len)
        grad_out = jnp.sum(packed[:, 2 * seq_len :], axis=0)

        d_pre = (slope_all.astype(jnp.float32) * flat_all[:, None]).astype(jnp.bfloat16)
        contract = (((0,), (0,)), ((), ()))
        grad_in = lax.dot_general(columns, d_pre, contract, preferred_element_type=jnp.float32)

        own_vocab = vocab_size // n_dp
        ids_perm = ids_all.reshape(n_dp, n_tensor, rows).transpose(1, 0, 2).reshape(-1)
        spot = ids_perm - me * own_vocab
        lines = -(-own_vocab // 128)
        inside = (spot >= 0) & (spot < own_vocab)
        line = jnp.where(inside, spot // 128, -1)
        high = jnp.where(jnp.arange(lines)[:, None] == line[None, :], flat_all[None, :], 0.0)
        low = (jnp.arange(128)[None, :] == (spot % 128)[:, None]).astype(jnp.float32)
        grad_bias = jnp.dot(high, low, precision=lax.Precision.HIGHEST)
        grad_bias = grad_bias.reshape(-1)[:own_vocab]
        return (twist_vals, grad_in, grad_out, grad_bias)

    return local


def solution(mesh):
    placed = (
        P("dp"),
        P("dp", "tensor"),
        P("tensor", None),
        P(("dp", "tensor"), None),
        P(),
        P("dp", "tensor"),
        P("tensor"),
        P(),
        P("dp"),
        P("dp"),
    )
    return jax.shard_map(
        make_local(mesh.shape["dp"], mesh.shape["tensor"]),
        mesh=mesh,
        in_specs=placed,
        out_specs=(P("dp"), P("dp", "tensor"), P("tensor"), P("dp")),
        check_vma=False,
    )
```
